32 devices in a mesh: groups: 2 (over y), row: 8 (over z, x), col: 2 (over core).
Axes of the slice: x: 2, y: 2, z: 4, core: 2. Of those that a mesh axis runs over, the one named last changes fastest.
Arguments:
- coeffs: float32 [16384, 128], P(('groups', 'row')), parts along dimension 0, may hold values from -0.4 to 0.4
- blocks: float32 [4096, 4096], P(('groups', 'row')), parts along dimension 0, may hold values from -0.75 to 0.75
- block_list: int32 [4096, 2], P(('groups', 'row')), parts along dimension 0, may hold values from 0 to 127
- block_count: int32 [16], P(('groups', 'row')), parts along dimension 0, may hold values from 32 to 256, as said below
Outputs:
- exchange_out: float32 [16384, 128], P(('groups', 'row', 'col')), parts along dimension 0
The draws below stay inside these ranges and needn't reach their ends.
There are 2 independent parts, one for each index of `groups`. The reference program is written for one: setup_inputs(seed, part) draws one part's arguments, and reference() takes and returns one part's arrays. A program takes and returns all parts, laid end to end along the dimension named above; each array names one. Nothing has to cross between parts.
Inputs may be any that keep to these rules, and one draw needn't show every extreme that they name: Only the first block_count[p] slots of fitting function p are screened in; some fitting function fills all 256 slots.
All inputs are finite; a program needn't handle non-finite values.
Results may differ from the reference program's by a relative error of at most 0.0003.
Values sent between devices are 32-bit elements; how exact they have to be, the bound alone decides.
A program may use at most 64 MiB of HBM per device.

```python
import jax
import jax.numpy as jnp
from jax import lax

NBAS = 8192
NOCC = 128
BLK = 64
NBLK = 256
NFIT = 8


def draw_block_count(key, part):
    key = jax.random.fold_in(key, 7)
    first_key, second_key = jax.random.split(key)
    spread = NBLK // 8 + jax.random.randint(first_key, (NFIT,), 0, NBLK // 2)
    busiest = jax.random.randint(second_key, (), 0, NFIT)
    return jnp.where(jnp.arange(NFIT) == busiest, NBLK, spread).astype(jnp.int32)


def place_ends(result, key, least, high):
    index_at = [jax.random.randint(jax.random.fold_in(key, axis), (), 0, length) for axis, length in enumerate(result.shape)]
    widest = result.shape.index(max(result.shape))
    neighbour = index_at[:widest] + [(index_at[widest] + 1) % result.shape[widest]] + index_at[widest + 1:]
    return result.at[tuple(index_at)].set(least).at[tuple(neighbour)].set(high)


def block_scale(rng, shape, cuts, least, largest):
    def one(dim, parts):
        heights = jax.random.uniform(jax.random.fold_in(jax.random.fold_in(rng, 6), dim), (parts,), jnp.float32, least / len(cuts), largest / len(cuts))
        return jnp.repeat(jnp.exp(heights), shape[dim] // parts).reshape((-1,) + (1,) * (len(shape) - dim - 1))

    level = one(*cuts[0])
    for cut in cuts[1:]:
        level = level * one(*cut)
    return level


def noise(key, shape, scale, reach, cuts=(), held_as=jnp.bfloat16):
    gain = block_scale(key, shape, cuts, -0.22, 0.18) if cuts else 1.0
    entries = jax.random.normal(key, shape, jnp.float32) * scale * gain
    return jnp.minimum(jnp.maximum(entries, -reach), reach).astype(held_as)


def setup_inputs(seed: int = 0, part: int = 0) -> dict:
    streams_of = jax.random.split(jax.random.key(seed), 5)
    part_splits = jax.random.split(jax.random.fold_in(streams_of[4], part), 5)
    return {
        "coeffs": noise(part_splits[0], (NBAS, NOCC), 0.05, 0.4, ((0, 8),), jnp.float32),
        "blocks": noise(part_splits[1], (NFIT * NBLK, BLK * BLK), BLK ** -0.5, 0.75, ((0, 8),), jnp.float32),
        "block_list": place_ends(jax.random.randint(part_splits[2], (NFIT * NBLK, 2), 0, NBAS // BLK), jax.random.fold_in(part_splits[2], 1), 0, (NBAS // BLK) - 1).astype(jnp.int32),
        "block_count": draw_block_count(jax.random.fold_in(jax.random.fold_in(streams_of[4], part), 71), part),
    }


def half_transform(block_set, pair_set, live_count, coeff_table):
    in_use = (jnp.arange(block_set.shape[0]) < live_count).astype(jnp.float32)
    picked = coeff_table[pair_set[:, 1]]
    product = jnp.einsum('sml,slj->smj', block_set, picked, precision=lax.Precision.HIGHEST)
    product = product * in_use[:, None, None]
    summed = jax.ops.segment_sum(product, pair_set[:, 0], num_segments=NBAS // BLK)
    return summed.reshape(NBAS, NOCC)


def reference(coeffs, blocks, block_list, block_count):
    coeff_table = coeffs.reshape(NBAS // BLK, BLK, NOCC)
    stacked = blocks.reshape(NFIT, NBLK, BLK, BLK)
    pair_table = block_list.reshape(NFIT, NBLK, 2)

    def advance(running, inputs):
        block_set, pair_set, live_count = inputs
        slab = half_transform(block_set, pair_set, live_count, coeff_table)
        projected = jnp.dot(slab.T, coeffs, precision=lax.Precision.HIGHEST, preferred_element_type=jnp.float32)
        running = running + jnp.dot(slab, projected, precision=lax.Precision.HIGHEST, preferred_element_type=jnp.float32)
        return running, None

    running, unused = lax.scan(advance, jnp.zeros((NBAS, NOCC), jnp.float32), (stacked, pair_table, block_count))
    return running
```

```python
import jax
import jax.numpy as jnp
from jax import lax
from jax.experimental import pallas as pl
from jax.experimental.pallas import tpu as pltpu
from jax.sharding import PartitionSpec as P

BLK = 64
LINE = 4
F32 = jnp.float32
BF16 = jnp.bfloat16


def split(value):
    high = value.astype(BF16)
    low = (value - high.astype(F32)).astype(BF16)
    return high, low


def mul(a, b):
    return jnp.dot(a, b, preferred_element_type=F32)


def mul_t(a, b):
    return lax.dot_general(a, b, (((0,), (0,)), ((), ())), preferred_element_type=F32)


def kernel(
    columns, rows, count, coeffs, blocks, out,
    full, tiles, pieces, table, prod, slab, proj, pbd, pbl,
    own, sib_out, sib_in, x_in, up_in, dn_in,
    blk_sem, ag_line, ag_x, ag_sib, rs_sib, rs_x, rs_line,
):
    row = lax.axis_index("row")
    z, x, c = lax.div(row, 2), lax.rem(row, 2), lax.axis_index("col")
    shard = coeffs.shape[0]
    half = shard // 2
    segs = full.shape[0] // BLK
    slots = blocks.shape[0]
    lanes = 128
    kk = blocks.shape[1] // lanes
    chunk = half // 2
    has_dn, has_up = z > 0, z < LINE - 1

    def send(src, dst, send_sem, recv_sem, where):
        return pltpu.make_async_remote_copy(
            src_ref=src, dst_ref=dst, send_sem=send_sem, recv_sem=recv_sem,
            device_id=where, device_id_type=pl.DeviceIdType.MESH,
        )

    up, down, across, mate = {"row": row + 2}, {"row": row - 2}, {"row": row + 1 - 2 * x}, {"col": 1 - c}

    def fetch(k):
        return pltpu.make_async_copy(
            blocks.at[:, pl.ds(k * lanes, lanes)], tiles.at[pl.ds(k * slots, slots), :], blk_sem.at[k]
        )

    for k in range(kk):
        fetch(k).start()

    barrier = pltpu.get_barrier_semaphore()

    def greet(where):
        pl.semaphore_signal(barrier, inc=1, device_id=where, device_id_type=pl.DeviceIdType.MESH)

    greet(across)
    greet(mate)
    pl.when(has_up)(lambda: greet(up))
    pl.when(has_dn)(lambda: greet(down))
    pl.semaphore_wait(barrier, 2 + lax.div(z + LINE - 2, LINE - 1) + lax.div(2 * LINE - 3 - z, LINE - 1))

    def piece(zz, xx, cc):
        start = (zz * 2 + xx) * shard + cc * half
        return full.at[pl.ds(pl.multiple_of(start, half), half), :]

    def line_copy(way, step, zz, src=None):
        here = piece(zz, x, c)
        return send(here if src is None else src, here, ag_line.at[0, way, step], ag_line.at[1, way, step],
                    up if way == 0 else down)

    def x_copy(zz, src=None, xx=None):
        here = piece(zz, x if xx is None else xx, c)
        return send(here if src is None else src, here, ag_x.at[0, zz], ag_x.at[1, zz], across)

    def sib_copy(zz, xx, cc):
        here = piece(zz, xx, cc)
        return send(here, here, ag_sib.at[0, zz * 2 + xx], ag_sib.at[1, zz * 2 + xx], mate)

    mine = coeffs.at[pl.ds(pl.multiple_of(c * half, half), half), :]
    pl.when(has_up)(lambda: line_copy(0, 0, z, mine).start())
    pl.when(has_dn)(lambda: line_copy(1, 0, z, mine).start())
    x_copy(z, mine).start()

    full[pl.ds(pl.multiple_of(row * shard, shard), shard), :] = coeffs[...]

    left = lax.broadcasted_iota(jnp.int32, (BLK, lanes), 1) < BLK

    def build(zz, xx, cc):
        first = (zz * 2 + xx) * (shard // BLK) + cc * (half // BLK)

        def one(q, carry):
            seg = first + q
            value = full[pl.ds(pl.multiple_of(seg * BLK, BLK), BLK), :]
            turned = pltpu.roll(value, BLK, 1)
            flag = jnp.broadcast_to(c, (BLK, lanes)) == 0
            top = jnp.where(left, jnp.where(flag, value, turned), 0.0)
            bottom = jnp.where(left, 0.0, jnp.where(flag, turned, value))
            table[seg, :BLK, :lanes], table[seg, :BLK, lanes:] = split(top)
            table[seg, BLK:, :lanes], table[seg, BLK:, lanes:] = split(bottom)
            return carry

        lax.fori_loop(0, half // BLK, one, 0, unroll=UNROLL_TABLE)

    def prepare(first, last):
        def one(s, carry):
            high, low = split(tiles[pl.ds(s, kk, stride=slots), :])
            pieces[s, :kk, :] = high
            pieces[s, kk:, :] = low
            return carry

        lax.fori_loop(first, last, one, 0, unroll=UNROLL_PREP)

    for k in range(kk):
        fetch(k).wait()
    prepare(0, slots // 2)
    build(z, x, 0)
    build(z, x, 1)

    def arrived(way, step):
        zz = z - step if way == 0 else z + step

        @pl.when(z >= step if way == 0 else z + step < LINE)
        def _():
            line_copy(way, step - 1, zz).wait_recv()
            if step < LINE - 1:
                pl.when(has_up if way == 0 else has_dn)(lambda: line_copy(way, step, zz).start())
            x_copy(zz).start()
            sib_copy(zz, x, c).start()
        return zz

    def exists(way, step, act):
        zz = z - step if way == 0 else z + step
        pl.when(z >= step if way == 0 else z + step < LINE)(lambda: act(zz))

    def crossed(zz):
        x_copy(zz, xx=1 - x).wait_recv()
        sib_copy(zz, 1 - x, c).start()

    def build_line(zz):
        build(zz, x, c)

    def build_far(zz):
        build(zz, 1 - x, c)

    def build_mate(zz):
        sib_copy(zz, x, 1 - c).wait_recv()
        build(zz, x, 1 - c)

    def build_mate_far(zz):
        sib_copy(zz, 1 - x, 1 - c).wait_recv()
        build(zz, 1 - x, 1 - c)

    for step in range(1, LINE + 1):
        if step < LINE:
            for way in (0, 1):
                arrived(way, step)
        if step == 1:
            crossed(z)
            prepare(slots // 2, slots)
            build_far(z)
        else:
            for way in (0, 1):
                exists(way, step - 1, crossed)
            for way in (0, 1):
                exists(way, step - 1, build_far)
        if step < LINE:
            for way in (0, 1):
                exists(way, step, build_line)
            for way in (0, 1):
                exists(way, step, build_mate)
        if step == 2:
            build_mate_far(z)
        if step > 2:
            for way in (0, 1):
                exists(way, step - 2, build_mate_far)
    for way in (0, 1):
        exists(way, LINE - 1, build_mate_far)

    def slot(s, carry):
        value = mul(pieces[s], table[columns[s]])
        low = value[kk:, :lanes] + value[kk:, lanes:]
        prod[pl.ds(s, kk, stride=slots), :] = value[:kk, :lanes] + (value[:kk, lanes:] + low)
        return carry

    lax.fori_loop(0, slots, slot, 0, unroll=UNROLL_SLOT)

    at_seg = lax.broadcasted_iota(jnp.int32, (segs, slots), 0) == rows[...]
    in_use = lax.broadcasted_iota(jnp.int32, (segs, slots), 1) < count[...]
    select = jnp.where(at_seg & in_use, 1.0, 0.0).astype(BF16)
    proj[...] = jnp.zeros_like(proj)

    def assemble(k, carry):
        high, low = split(prod[pl.ds(pl.multiple_of(k * slots, slots), slots), :])
        both = mul(select, jnp.concatenate([high, low], axis=1))
        part = both[:, :lanes] + both[:, lanes:]
        slab[pl.ds(k, segs, stride=kk), :] = part
        part_high, part_low = split(part)
        pair = jnp.concatenate(
            [full[pl.ds(2 * k, segs, stride=BLK), :], full[pl.ds(2 * k + 1, segs, stride=BLK), :]], axis=1
        )
        pair_high, pair_low = split(pair)
        proj[...] += mul_t(
            jnp.concatenate([part_high, part_low], axis=0), jnp.concatenate([pair_high, pair_high], axis=0)
        ) + mul_t(part_high, pair_low)
        return carry

    lax.fori_loop(0, kk, assemble, 0, unroll=UNROLL_ASM)

    projected = proj[:BLK, :lanes] + proj[BLK:, lanes:]
    high, low = split(projected)
    blank = jnp.zeros((BLK, lanes), BF16)
    for base in (0, 2 * BLK):
        pbd[base:base + BLK, :lanes] = high
        pbd[base:base + BLK, lanes:] = blank
        pbd[base + BLK:base + 2 * BLK, :lanes] = blank
        pbd[base + BLK:base + 2 * BLK, lanes:] = high
    pbl[:BLK, :lanes] = low
    pbl[:BLK, lanes:] = blank
    pbl[BLK:, :lanes] = blank
    pbl[BLK:, lanes:] = low

    def value_of(zz, xx, cc):
        start = (zz * 2 + xx) * 2 * chunk + cc * chunk
        high, low = split(slab[pl.ds(pl.multiple_of(start, chunk), chunk), :])
        return mul(jnp.concatenate([high, low], axis=1), pbd[...]) + mul(high, pbl[...])

    side, mirror = lax.div(z, 2), z + lax.div(z, 2) * (LINE - 1 - 2 * z)

    def flip(value):
        return value + side * (LINE - 1 - 2 * value)

    order = [flip(jnp.int32(3)), flip(jnp.int32(2)), flip(1 - mirror), flip(mirror)]

    def mate_copy(d, e):
        at = d * 2 + e
        return send(sib_out.at[at], sib_in.at[at], rs_sib.at[0, at], rs_sib.at[1, at], mate)

    def cross_copy(d):
        return send(own.at[d * 2 + 1 - x], x_in.at[d], rs_x.at[0, d], rs_x.at[1, d], across)

    def up_copy(d):
        return send(own.at[d * 2 + x], up_in.at[d], rs_line.at[0, 0, d], rs_line.at[1, 0, d], up)

    def dn_copy(d):
        return send(own.at[d * 2 + x], dn_in.at[d], rs_line.at[0, 1, d], rs_line.at[1, 1, d], down)

    def to_mate(d, e):
        sib_out[d * 2 + e] = value_of(d, e, 1 - c)
        mate_copy(d, e).start()

    def keep(d, e):
        own[d * 2 + e] = value_of(d, e, c)

    def add_mate(d, e):
        mate_copy(d, e).wait_recv()
        own[d * 2 + e] += sib_in[d * 2 + e]

    to_mate(order[0], 1 - x)
    for i in range(LINE):
        d = order[i]
        keep(d, 1 - x)
        if i + 1 < LINE:
            to_mate(order[i + 1], 1 - x)
        else:
            to_mate(order[0], x)
        add_mate(d, 1 - x)
        cross_copy(d).start()
    for i in range(LINE):
        d = order[i]
        keep(d, x)
        if i + 1 < LINE:
            to_mate(order[i + 1], x)
        add_mate(d, x)
    for i in range(LINE - 1):
        d = order[i]
        cross_copy(d).wait_recv()
        own[d * 2 + x] += x_in[d]

        @pl.when(d > z)
        def _():
            @pl.when(has_dn)
            def _():
                up_copy(d).wait_recv()
                own[d * 2 + x] += up_in[d]
            up_copy(d).start()

        @pl.when(d < z)
        def _():
            @pl.when(has_up)
            def _():
                dn_copy(d).wait_recv()
                own[d * 2 + x] += dn_in[d]
            dn_copy(d).start()

    cross_copy(z).wait_recv()
    own[z * 2 + x] += x_in[z]

    @pl.when(has_dn)
    def _():
        up_copy(z).wait_recv()
        own[z * 2 + x] += up_in[z]

    @pl.when(has_up)
    def _():
        dn_copy(z).wait_recv()
        own[z * 2 + x] += dn_in[z]

    out[pl.ds(0, chunk, stride=2), :] = own[z * 2 + x, :, :lanes]
    out[pl.ds(1, chunk, stride=2), :] = own[z * 2 + x, :, lanes:]

    for way in (0, 1):
        edge = has_up if way == 0 else has_dn
        pl.when(edge)(lambda way=way: line_copy(way, 0, z, mine).wait_send())
        for step in range(1, LINE):
            def done(zz, way=way, step=step, edge=edge):
                if step < LINE - 1:
                    pl.when(edge)(lambda: line_copy(way, step, zz).wait_send())
                x_copy(zz).wait_send()
                sib_copy(zz, x, c).wait_send()
                sib_copy(zz, 1 - x, c).wait_send()
            exists(way, step, done)
    x_copy(z, mine).wait_send()
    sib_copy(z, 1 - x, c).wait_send()
    for d in range(LINE):
        for e in (0, 1):
            mate_copy(d, e).wait_send()
        cross_copy(d).wait_send()
        pl.when(d > z)(lambda d=d: up_copy(d).wait_send())
        pl.when(d < z)(lambda d=d: dn_copy(d).wait_send())


UNROLL_TABLE = 2
UNROLL_PREP = 8
UNROLL_SLOT = 8
UNROLL_ASM = 2


def exchange(coeffs, blocks, block_list, block_count):
    shard, occupied = coeffs.shape
    slots, flat = blocks.shape
    total = shard * lax.axis_size("row")
    half = shard // 2
    chunk = half // 2
    lanes = 128
    kk = flat // lanes
    segs = total // BLK
    listed = block_list.T
    wide = 2 * lanes
    vmem = pl.BlockSpec(memory_space=pltpu.VMEM)
    dma = pltpu.SemaphoreType.DMA
    return pl.pallas_call(
        kernel,
        out_shape=jax.ShapeDtypeStruct((half, occupied), F32),
        in_specs=[
            pl.BlockSpec(memory_space=pltpu.SMEM), vmem, vmem, vmem, pl.BlockSpec(memory_space=pl.ANY),
        ],
        out_specs=vmem,
        scratch_shapes=[
            pltpu.VMEM((total, occupied), F32),
            pltpu.VMEM((slots * kk, lanes), F32),
            pltpu.VMEM((slots, 2 * kk, lanes), BF16),
            pltpu.VMEM((segs, 2 * BLK, wide), BF16),
            pltpu.VMEM((slots * kk, lanes), F32),
            pltpu.VMEM((segs * kk, lanes), F32),
            pltpu.VMEM((lanes, wide), F32),
            pltpu.VMEM((2 * lanes, wide), BF16),
            pltpu.VMEM((lanes, wide), BF16),
            pltpu.VMEM((2 * LINE, chunk, wide), F32),
            pltpu.VMEM((2 * LINE, chunk, wide), F32),
            pltpu.VMEM((2 * LINE, chunk, wide), F32),
            pltpu.VMEM((LINE, chunk, wide), F32),
            pltpu.VMEM((LINE, chunk, wide), F32),
            pltpu.VMEM((LINE, chunk, wide), F32),
            dma((kk,)),
            dma((2, 2, LINE - 1)),
            dma((2, LINE)),
            dma((2, 2 * LINE)),
            dma((2, 2 * LINE)),
            dma((2, LINE)),
            dma((2, 2, LINE)),
        ],
        compiler_params=pltpu.CompilerParams(
            collective_id=0, has_side_effects=True, vmem_limit_bytes=56 * 1024 * 1024
        ),
    )(listed[1], listed[:1], block_count[:, None], coeffs, blocks)


def plain(coeffs, blocks, block_list, block_count):
    full_coeffs = lax.all_gather(coeffs, "row", axis=0, tiled=True)
    total_rows, occupied = full_coeffs.shape
    half_width = occupied // lax.axis_size("col")
    halves = lax.dynamic_slice_in_dim(
        full_coeffs, lax.axis_index("col") * half_width, half_width, 1
    )
    block_edge = BLK
    segments = total_rows // block_edge
    coeff_table = halves.reshape(segments, block_edge, half_width)
    slot_total = blocks.shape[0]
    group_size = slot_total // 4
    live_count = block_count[0]
    group_count = (live_count + group_size - 1) // group_size

    def accumulate(round_index, slab_table):
        first_slot = round_index * group_size
        chosen = lax.dynamic_slice_in_dim(block_list, first_slot, group_size, 0)
        pieces = lax.dynamic_slice_in_dim(blocks, first_slot, group_size, 0).reshape(
            group_size, block_edge, block_edge
        )
        picked = coeff_table[chosen[:, 1]]
        product = jnp.einsum(
            "sml,slj->smj",
            pieces,
            picked,
            precision=lax.Precision.HIGHEST,
            preferred_element_type=jnp.float32,
        )
        in_use = first_slot + jnp.arange(group_size) < live_count
        row_select = (
            (chosen[:, 0][None, :] == jnp.arange(segments)[:, None]) & in_use[None, :]
        ).astype(jnp.float32)
        flat_product = product.reshape(group_size, block_edge * half_width)
        return slab_table + jnp.dot(
            row_select,
            flat_product,
            precision=lax.Precision.HIGHEST,
            preferred_element_type=jnp.float32,
        )

    slab_table = lax.fori_loop(
        0, group_count, accumulate, jnp.zeros((segments, block_edge * half_width), jnp.float32)
    )
    slab = slab_table.reshape(total_rows, half_width)
    projected = jnp.dot(
        slab.T, full_coeffs, precision=lax.Precision.HIGHEST, preferred_element_type=jnp.float32
    )
    arrived_slabs = lax.all_to_all(slab[None], "row", split_axis=1, concat_axis=0, tiled=True)
    partial_value = jnp.einsum(
        "pmj,pji->mi",
        arrived_slabs,
        lax.all_gather(projected[None], "row", axis=0, tiled=True),
        precision=lax.Precision.HIGHEST,
        preferred_element_type=jnp.float32,
    )
    return lax.psum_scatter(partial_value, "col", scatter_dimension=0, tiled=True)


def body(coeffs, blocks, block_list, block_count):
    if lax.axis_size("row") == 2 * LINE and lax.axis_size("col") == 2:
        return exchange(coeffs, blocks, block_list, block_count)
    return plain(coeffs, blocks, block_list, block_count)


def solution(mesh):
    in_specs = (
        P(("groups", "row"), None),
        P(("groups", "row"), None),
        P(("groups", "row"), None),
        P(("groups", "row")),
    )
    out_specs = P(("groups", "row", "col"), None)
    return jax.shard_map(body, mesh=mesh, in_specs=in_specs, out_specs=out_specs, check_vma=False)
```
